32 devices in a mesh: groups: 2 (over y), gx: 8 (over z, x), gy: 2 (over core).
Axes of the slice: x: 2, y: 2, z: 4, core: 2. Of those that a mesh axis runs over, the one named last changes fastest.
Arguments:
- activations: bfloat16 [1024, 2, 4096], P('groups', 'gy', 'gx'), parts along dimension 0, may hold values from -6 to 6
- gate_weight: bfloat16 [8192, 26624], P('gy', 'gx'), may hold values from -0.0625 to 0.0625
- up_weight: bfloat16 [8192, 26624], P('gy', 'gx'), may hold values from -0.0625 to 0.0625
Outputs:
- hidden: bfloat16 [1024, 26624], P(('groups', 'gy'), 'gx'), parts along dimension 0
The draws below stay inside these ranges and needn't reach their ends.
There are 2 independent parts, one for each index of `groups`. The reference program is written for one: setup_inputs(seed, part) draws one part's arguments, and reference() takes and returns one part's arrays. A program takes and returns all parts, laid end to end along the dimension named above; an argument that names none is the same for every part. Nothing has to cross between parts.
All inputs are finite; a program needn't handle non-finite values.
Results may differ from the reference program's by a relative error of at most 0.001.
Values may be sent and summed in bfloat16 or wider, within the bound.
A program may use at most 320 MiB of HBM per device.

```python
import jax
import jax.numpy as jnp

D = 8192
FF = 26624
ROWS = 512
N_GY = 2


def level_of(own_key, extent, split, smallest, top_value):
    def one(position, blocks):
        heights = jax.random.uniform(jax.random.fold_in(jax.random.fold_in(own_key, 6), position), (blocks,), jnp.float32, smallest / len(split), top_value / len(split))
        return jnp.repeat(jnp.exp(heights), extent[position] // blocks).reshape((-1,) + (1,) * (len(extent) - position - 1))

    level = one(*split[0])
    for cut in split[1:]:
        level = level * one(*cut)
    return level


def gaussian(own_key, shape, scale, most, shards=(), dtype=jnp.bfloat16):
    loudness = level_of(own_key, shape, shards, -0.22, 0.18) if shards else 1.0
    drawn = jax.random.normal(own_key, shape, jnp.float32) * scale * loudness
    return jnp.minimum(jnp.maximum(drawn, -most), most).astype(dtype)


def setup_inputs(seed: int = 0, part: int = 0) -> dict:
    arg_keys = jax.random.split(jax.random.key(seed), 4)
    part_splits = jax.random.split(jax.random.fold_in(arg_keys[3], part), 4)
    activations = gaussian(part_splits[0], (ROWS, N_GY, D // N_GY), 1.0, 6.0, ((1, 2), (2, 8)))
    gate_weight = gaussian(arg_keys[1], (D, FF), D ** -0.5, 0.0625, ((0, 2), (1, 8)))
    up_weight = gaussian(arg_keys[2], (D, FF), D ** -0.5, 0.0625, ((0, 2), (1, 8)))
    return {"activations": activations, "gate_weight": gate_weight, "up_weight": up_weight}


def reference(activations, gate_weight, up_weight):
    features = activations.reshape(activations.shape[0], -1)
    gate = jnp.dot(features, gate_weight, preferred_element_type=jnp.float32)
    up = jnp.dot(features, up_weight, preferred_element_type=jnp.float32)
    return (jax.nn.silu(gate) * up).astype(jnp.bfloat16)
```

```python
import functools

import jax
import jax.numpy as jnp
from jax import lax
from jax.experimental import pallas as pl
from jax.experimental.pallas import tpu as pltpu
from jax.sharding import PartitionSpec as P

MESH = pl.DeviceIdType.MESH
PLANES = 4
CHUNKS = 4
TILE = 256


def gated(gate, up):
    return (jax.nn.silu(gate) * up).astype(jnp.bfloat16)


def shards(activations, gate_weight, up_weight):
    rows = activations.shape[0]
    piece = lax.all_gather(activations, "gx", axis=2, tiled=True)
    count = piece.shape[2]
    flat = piece.reshape(rows, count)
    gate = jnp.dot(flat, gate_weight, preferred_element_type=jnp.float32)
    up = jnp.dot(flat, up_weight, preferred_element_type=jnp.float32)
    gate_rows, up_rows = (
        lax.psum_scatter(gate, "gy", scatter_dimension=0, tiled=True),
        lax.psum_scatter(up, "gy", scatter_dimension=0, tiled=True),
    )
    return gated(gate_rows, up_rows)


def kernel(act, wg, wu, out, x, bg, bu, acc, got, res,
           act_sem, w_sem, send_sem, recv_sem, ex_send, ex_recv, out_sem):
    rows, width = act.shape
    depth = 2 * width
    half = rows // 2
    size = rows // CHUNKS
    part = size // 2
    tiles = acc.shape[0]
    gx = lax.axis_index("gx")
    c = lax.axis_index("gy")
    z = gx // 2
    col = gx % 2
    near = (PLANES - 1 - z) // 2
    p1 = z - 1 + 2 * near
    p3 = (PLANES - 1) * near
    p2 = 6 - z - p1 - p3
    order = [z, p1, p2, p3]

    def own(r, h):
        return pltpu.make_async_copy(
            act.at[pl.ds(h * half + r * part, part), :],
            x.at[z, pl.ds(r * size + h * part, part), pl.ds(col * width, width)],
            act_sem.at[r, h],
        )

    for r in range(CHUNKS):
        for h in range(2):
            own(r, h).start()

    def weights(s):
        span = pl.ds(order[s] * depth, depth)
        return [
            pltpu.make_async_copy(wg.at[span, :], bg.at[s % 2], w_sem.at[0, s]),
            pltpu.make_async_copy(wu.at[span, :], bu.at[s % 2], w_sem.at[1, s]),
        ]

    for s in range(2):
        for copy in weights(s):
            copy.start()

    targets = [z * 2 + (1 - col), gx + 2, gx - 2]
    barrier = pltpu.get_barrier_semaphore()
    pl.semaphore_signal(barrier, inc=1, device_id={"gx": targets[0]}, device_id_type=MESH)
    pl.semaphore_signal(barrier, inc=1, device_id={"gy": 1 - c}, device_id_type=MESH)

    @pl.when(z < PLANES - 1)
    def _():
        pl.semaphore_signal(barrier, inc=1, device_id={"gx": targets[1]}, device_id_type=MESH)

    @pl.when(z > 0)
    def _():
        pl.semaphore_signal(barrier, inc=1, device_id={"gx": targets[2]}, device_id_type=MESH)

    pl.semaphore_wait(barrier, 2 + (z + 2) // 3 + (5 - z) // 3)

    def link(d, p, side, r):
        block = x.at[p, pl.ds(r * size, size), pl.ds(side * width, width)]
        b = p * 2 + side
        return pltpu.make_async_remote_copy(
            src_ref=block, dst_ref=block,
            send_sem=send_sem.at[d, b, r], recv_sem=recv_sem.at[b, r],
            device_id={"gx": targets[d]}, device_id_type=MESH,
        )

    def along(at, p, r):
        inner = ((at == 1) & (p == 0)) | ((at == 2) & (p == 3))
        outer = ((at == 0) & (p == 1)) | ((at == 3) & (p == 2))
        return inner | (outer & (r % 2 == 1))

    def routes(p, side_own, r):
        rise = (p <= z) & (z < PLANES - 1)
        fall = (p >= z) & (z > 0)
        if side_own:
            return [(1, rise), (2, fall), (0, jnp.logical_not(along(z, p, r)))]
        return [(1, rise & along(z + 1, p, r)), (2, fall & along(z - 1, p, r))]

    def forward(p, side_own, r, wait=False):
        side = col if side_own else 1 - col
        for d, cond in routes(p, side_own, r):
            @pl.when(cond)
            def _(d=d):
                if wait:
                    link(d, p, side, r).wait_send()
                else:
                    link(d, p, side, r).start()

    def arrive(p, side_own, r):
        link(0, p, col if side_own else 1 - col, r).wait_recv()

    for r in range(CHUNKS):
        for h in range(2):
            own(r, h).wait()
        forward(z, True, r)

    def product(s, first, count, j):
        lhs = x[order[s], pl.ds(first, count), :]
        cut = pl.ds(pl.multiple_of(j * TILE, TILE), TILE)
        gate = jnp.dot(lhs, bg[s % 2, :, cut], preferred_element_type=jnp.float32)
        up = jnp.dot(lhs, bu[s % 2, :, cut], preferred_element_type=jnp.float32)
        return gate, up

    def accumulate(s, first, count):
        here = pl.ds(first, count)

        def body(j, carry):
            gate, up = product(s, first, count, j)
            if s:
                acc[j, here, :TILE] += gate
                acc[j, here, TILE:] += up
            else:
                acc[j, here, :TILE] = gate
                acc[j, here, TILE:] = up
            return carry

        lax.fori_loop(0, tiles, body, 0)

    def exchange(r, j):
        return pltpu.make_async_remote_copy(
            src_ref=acc.at[j, pl.ds(r * size + (1 - c) * part, part), :],
            dst_ref=got.at[j, pl.ds(r * part, part), :],
            send_sem=ex_send.at[j, r], recv_sem=ex_recv.at[j, r],
            device_id={"gy": 1 - c}, device_id_type=MESH,
        )

    def write(r):
        span = pl.ds(r * part, part)
        return pltpu.make_async_copy(res.at[span, :], out.at[span, :], out_sem.at[r])

    def finish(r):
        def body(j, carry):
            exchange(r, j).wait_recv()
            both = acc[j, pl.ds(r * size + c * part, part), :] + got[j, pl.ds(r * part, part), :]
            cut = pl.ds(pl.multiple_of(j * TILE, TILE), TILE)
            res[pl.ds(r * part, part), cut] = gated(both[:, :TILE], both[:, TILE:])
            return carry

        lax.fori_loop(0, tiles, body, 0)
        write(r).start()

    group = 2
    for s in range(PLANES):
        for copy in weights(s):
            copy.wait()

        def chunk(r, carry, s=s):
            if s < PLANES - 1:
                arrive(order[s + 1], True, r)
                forward(order[s + 1], True, r)
            arrive(order[s], False, r)
            forward(order[s], False, r)
            return carry

        if s < PLANES - 1:
            def block(k, carry, s=s):
                for i in range(group):
                    chunk(k * group + i, 0, s)
                accumulate(s, pl.multiple_of(k * group * size, size), group * size)
                return carry

            lax.fori_loop(0, CHUNKS // group, block, 0)
            if s + 2 < PLANES:
                for copy in weights(s + 2):
                    copy.start()
        else:
            def last(r, carry, s=s):
                chunk(r, 0, s)
                accumulate(s, pl.multiple_of(r * size, size), size)

                def push(j, carry):
                    exchange(r, j).start()
                    return carry

                lax.fori_loop(0, tiles, push, 0)

                @pl.when(r > 0)
                def _():
                    finish(r - 1)
                return carry

            lax.fori_loop(0, CHUNKS, last, 0)
            finish(CHUNKS - 1)

    def drain(r, carry):
        for s in range(PLANES):
            forward(order[s], True, r, wait=True)
            forward(order[s], False, r, wait=True)

        def body(j, carry):
            exchange(r, j).wait_send()
            return carry

        lax.fori_loop(0, tiles, body, 0)
        write(r).wait()
        return carry

    lax.fori_loop(0, CHUNKS, drain, 0)


def fused(activations, gate_weight, up_weight):
    rows, _, width = activations.shape
    hidden = gate_weight.shape[1]
    tiles = hidden // TILE
    depth = 2 * width
    return pl.pallas_call(
        kernel,
        out_shape=jax.ShapeDtypeStruct((rows // 2, hidden), jnp.bfloat16),
        in_specs=[pl.BlockSpec(memory_space=pl.ANY)] * 3,
        out_specs=pl.BlockSpec(memory_space=pl.ANY),
        scratch_shapes=[
            pltpu.VMEM((PLANES, rows, depth), jnp.bfloat16),
            pltpu.VMEM((2, depth, hidden), jnp.bfloat16),
            pltpu.VMEM((2, depth, hidden), jnp.bfloat16),
            pltpu.VMEM((tiles, rows, 2 * TILE), jnp.float32),
            pltpu.VMEM((tiles, rows // 2, 2 * TILE), jnp.float32),
            pltpu.VMEM((rows // 2, hidden), jnp.bfloat16),
            pltpu.SemaphoreType.DMA((CHUNKS, 2)),
            pltpu.SemaphoreType.DMA((2, PLANES)),
            pltpu.SemaphoreType.DMA((3, 2 * PLANES, CHUNKS)),
            pltpu.SemaphoreType.DMA((2 * PLANES, CHUNKS)),
            pltpu.SemaphoreType.DMA((tiles, CHUNKS)),
            pltpu.SemaphoreType.DMA((tiles, CHUNKS)),
            pltpu.SemaphoreType.DMA((CHUNKS,)),
        ],
        compiler_params=pltpu.CompilerParams(
            collective_id=0, has_side_effects=True, vmem_limit_bytes=62 * 1024 * 1024
        ),
        cost_estimate=pl.CostEstimate(
            flops=4 * rows * PLANES * depth * hidden,
            bytes_accessed=4 * PLANES * depth * hidden,
            transcendentals=rows // 2 * hidden,
        ),
    )(activations.reshape(rows, width), gate_weight, up_weight)


def solution(mesh):
    def local(activations, gate_weight, up_weight):
        rows, _, width = activations.shape
        hidden = gate_weight.shape[1]
        fits = (
            mesh.shape["gx"] == 2 * PLANES and mesh.shape["gy"] == 2
            and width % 128 == 0 and hidden % TILE == 0 and rows % (32 * CHUNKS) == 0
        )
        return (fused if fits else shards)(activations, gate_weight, up_weight)

    placed = (P("groups", "gy", "gx"), P("gy", "gx"), P("gy", "gx"))
    return jax.shard_map(
        local, mesh=mesh, in_specs=placed, out_specs=P(("groups", "gy"), "gx"), check_vma=False
    )
```

```python
import functools

import jax
import jax.numpy as jnp
from jax import lax
from jax.experimental import pallas as pl
from jax.experimental.pallas import tpu as pltpu
from jax.sharding import PartitionSpec as P

MESH = pl.DeviceIdType.MESH
PLANES = 4
CHUNKS = 4
TILE = 256
SPAN = 5


def gated(gate, up):
    return (jax.nn.silu(gate) * up).astype(jnp.bfloat16)


def shards(activations, gate_weight, up_weight):
    rows = activations.shape[0]
    piece = lax.all_gather(activations, "gx", axis=2, tiled=True)
    count = piece.shape[2]
    flat = piece.reshape(rows, count)
    gate = jnp.dot(flat, gate_weight, preferred_element_type=jnp.float32)
    up = jnp.dot(flat, up_weight, preferred_element_type=jnp.float32)
    gate_rows, up_rows = (
        lax.psum_scatter(gate, "gy", scatter_dimension=0, tiled=True),
        lax.psum_scatter(up, "gy", scatter_dimension=0, tiled=True),
    )
    return gated(gate_rows, up_rows)


def kernel(act, wg, wu, out, x, bg, bu, acc, got, res,
           act_sem, w_sem, send_sem, recv_sem, ex_send, ex_recv, out_sem):
    rows, width = act.shape
    depth = 2 * width
    half = rows // 2
    size = rows // CHUNKS
    part = size // 2
    tiles = acc.shape[0]
    gx = lax.axis_index("gx")
    c = lax.axis_index("gy")
    z = gx // 2
    col = gx % 2
    near = (PLANES - 1 - z) // 2
    p1 = z - 1 + 2 * near
    p3 = (PLANES - 1) * near
    p2 = 6 - z - p1 - p3
    order = [z, p1, p2, p3]

    def own(r, h):
        return pltpu.make_async_copy(
            act.at[pl.ds(h * half + r * part, part), :],
            x.at[z, pl.ds(r * size + h * part, part), pl.ds(col * width, width)],
            act_sem.at[r, h],
        )

    for r in range(CHUNKS):
        for h in range(2):
            own(r, h).start()

    def weights(s):
        span = pl.ds(order[s] * depth, depth)
        return [
            pltpu.make_async_copy(wg.at[span, :], bg.at[s % 2], w_sem.at[0, s]),
            pltpu.make_async_copy(wu.at[span, :], bu.at[s % 2], w_sem.at[1, s]),
        ]

    for s in range(2):
        for copy in weights(s):
            copy.start()

    targets = [z * 2 + (1 - col), gx + 2, gx - 2]
    barrier = pltpu.get_barrier_semaphore()
    pl.semaphore_signal(barrier, inc=1, device_id={"gx": targets[0]}, device_id_type=MESH)
    pl.semaphore_signal(barrier, inc=1, device_id={"gy": 1 - c}, device_id_type=MESH)

    @pl.when(z < PLANES - 1)
    def _():
        pl.semaphore_signal(barrier, inc=1, device_id={"gx": targets[1]}, device_id_type=MESH)

    @pl.when(z > 0)
    def _():
        pl.semaphore_signal(barrier, inc=1, device_id={"gx": targets[2]}, device_id_type=MESH)

    pl.semaphore_wait(barrier, 2 + (z + 2) // 3 + (5 - z) // 3)

    def link(d, p, side, r):
        block = x.at[p, pl.ds(r * size, size), pl.ds(side * width, width)]
        b = p * 2 + side
        return pltpu.make_async_remote_copy(
            src_ref=block, dst_ref=block,
            send_sem=send_sem.at[d, b, r], recv_sem=recv_sem.at[b, r],
            device_id={"gx": targets[d]}, device_id_type=MESH,
        )

    def along(at, p, r):
        inner = ((at == 1) & (p == 0)) | ((at == 2) & (p == 3))
        outer = ((at == 0) & (p == 1)) | ((at == 3) & (p == 2))
        return inner | (outer & (r % 2 == 1))

    def routes(p, side_own, r):
        rise = (p <= z) & (z < PLANES - 1)
        fall = (p >= z) & (z > 0)
        if side_own:
            return [(1, rise), (2, fall), (0, jnp.logical_not(along(z, p, r)))]
        return [(1, rise & along(z + 1, p, r)), (2, fall & along(z - 1, p, r))]

    def forward(p, side_own, r, wait=False):
        side = col if side_own else 1 - col
        for d, cond in routes(p, side_own, r):
            @pl.when(cond)
            def _(d=d):
                if wait:
                    link(d, p, side, r).wait_send()
                else:
                    link(d, p, side, r).start()

    def arrive(p, side_own, r):
        link(0, p, col if side_own else 1 - col, r).wait_recv()

    for r in range(CHUNKS):
        for h in range(2):
            own(r, h).wait()
        forward(z, True, r)

    def accumulate(s, first, count, span):
        here = pl.ds(first, count)
        for j in span:
            lhs = x[order[s], here, :]
            cut = pl.ds(j * TILE, TILE)
            gate = jnp.dot(lhs, bg[s % 2, :, cut], preferred_element_type=jnp.float32)
            up = jnp.dot(lhs, bu[s % 2, :, cut], preferred_element_type=jnp.float32)
            if s:
                acc[j, here, :TILE] += gate
                acc[j, here, TILE:] += up
            else:
                acc[j, here, :TILE] = gate
                acc[j, here, TILE:] = up

    def exchange(r, j):
        return pltpu.make_async_remote_copy(
            src_ref=acc.at[j, pl.ds(r * size + (1 - c) * part, part), :],
            dst_ref=got.at[j, pl.ds(r * part, part), :],
            send_sem=ex_send.at[j, r], recv_sem=ex_recv.at[j, r],
            device_id={"gy": 1 - c}, device_id_type=MESH,
        )

    def write(r):
        span = pl.ds(r * part, part)
        return pltpu.make_async_copy(res.at[span, :], out.at[span, :], out_sem.at[r])

    def finish(r):
        def body(j, carry):
            exchange(r, j).wait_recv()
            both = acc[j, pl.ds(r * size + c * part, part), :] + got[j, pl.ds(r * part, part), :]
            cut = pl.ds(pl.multiple_of(j * TILE, TILE), TILE)
            res[pl.ds(r * part, part), cut] = gated(both[:, :TILE], both[:, TILE:])
            return carry

        lax.fori_loop(0, tiles, body, 0)
        write(r).start()

    group = 2
    for s in range(PLANES):
        for copy in weights(s):
            copy.wait()

        def chunk(r, carry, s=s):
            if s < PLANES - 1:
                arrive(order[s + 1], True, r)
                forward(order[s + 1], True, r)
            arrive(order[s], False, r)
            forward(order[s], False, r)
            return carry

        if s < PLANES - 1:
            def block(k, carry, s=s):
                for i in range(group):
                    chunk(k * group + i, 0, s)
                accumulate(s, pl.multiple_of(k * group * size, size), group * size, range(tiles))
                return carry

            lax.fori_loop(0, CHUNKS // group, block, 0)
            if s + 2 < PLANES:
                for copy in weights(s + 2):
                    copy.start()
        else:
            def last(r, carry, s=s):
                chunk(r, 0, s)
                def push(j, carry):
                    exchange(r, j).start()
                    return carry

                for lo in range(0, tiles, SPAN):
                    hi = min(lo + SPAN, tiles)
                    accumulate(s, pl.multiple_of(r * size, size), size, range(lo, hi))
                    lax.fori_loop(lo, hi, push, 0)

                @pl.when(r > 0)
                def _():
                    finish(r - 1)
                return carry

            lax.fori_loop(0, CHUNKS, last, 0)
            finish(CHUNKS - 1)

    def drain(r, carry):
        for s in range(PLANES):
            forward(order[s], True, r, wait=True)
            forward(order[s], False, r, wait=True)

        def body(j, carry):
            exchange(r, j).wait_send()
            return carry

        lax.fori_loop(0, tiles, body, 0)
        write(r).wait()
        return carry

    lax.fori_loop(0, CHUNKS, drain, 0)


def fused(activations, gate_weight, up_weight):
    rows, _, width = activations.shape
    hidden = gate_weight.shape[1]
    tiles = hidden // TILE
    depth = 2 * width
    return pl.pallas_call(
        kernel,
        out_shape=jax.ShapeDtypeStruct((rows // 2, hidden), jnp.bfloat16),
        in_specs=[pl.BlockSpec(memory_space=pl.ANY)] * 3,
        out_specs=pl.BlockSpec(memory_space=pl.ANY),
        scratch_shapes=[
            pltpu.VMEM((PLANES, rows, depth), jnp.bfloat16),
            pltpu.VMEM((2, depth, hidden), jnp.bfloat16),
            pltpu.VMEM((2, depth, hidden), jnp.bfloat16),
            pltpu.VMEM((tiles, rows, 2 * TILE), jnp.float32),
            pltpu.VMEM((tiles, rows // 2, 2 * TILE), jnp.float32),
            pltpu.VMEM((rows // 2, hidden), jnp.bfloat16),
            pltpu.SemaphoreType.DMA((CHUNKS, 2)),
            pltpu.SemaphoreType.DMA((2, PLANES)),
            pltpu.SemaphoreType.DMA((3, 2 * PLANES, CHUNKS)),
            pltpu.SemaphoreType.DMA((2 * PLANES, CHUNKS)),
            pltpu.SemaphoreType.DMA((tiles, CHUNKS)),
            pltpu.SemaphoreType.DMA((tiles, CHUNKS)),
            pltpu.SemaphoreType.DMA((CHUNKS,)),
        ],
        compiler_params=pltpu.CompilerParams(
            collective_id=0, has_side_effects=True, vmem_limit_bytes=62 * 1024 * 1024
        ),
        cost_estimate=pl.CostEstimate(
            flops=4 * rows * PLANES * depth * hidden,
            bytes_accessed=4 * PLANES * depth * hidden,
            transcendentals=rows // 2 * hidden,
        ),
    )(activations.reshape(rows, width), gate_weight, up_weight)


def solution(mesh):
    def local(activations, gate_weight, up_weight):
        rows, _, width = activations.shape
        hidden = gate_weight.shape[1]
        fits = (
            mesh.shape["gx"] == 2 * PLANES and mesh.shape["gy"] == 2
            and width % 128 == 0 and hidden % TILE == 0 and rows % (32 * CHUNKS) == 0
        )
        return (fused if fits else shards)(activations, gate_weight, up_weight)

    placed = (P("groups", "gy", "gx"), P("gy", "gx"), P("gy", "gx"))
    return jax.shard_map(
        local, mesh=mesh, in_specs=placed, out_specs=P(("groups", "gy"), "gx"), check_vma=False
    )
```

```python
import functools

import jax
import jax.numpy as jnp
from jax import lax
from jax.experimental import pallas as pl
from jax.experimental.pallas import tpu as pltpu
from jax.sharding import PartitionSpec as P

MESH = pl.DeviceIdType.MESH
PLANES = 4
CHUNKS = 4
TILE = 256
SPAN = 5


def gated(gate, up):
    return (jax.nn.silu(gate) * up).astype(jnp.bfloat16)


def shards(activations, gate_weight, up_weight):
    rows = activations.shape[0]
    piece = lax.all_gather(activations, "gx", axis=2, tiled=True)
    count = piece.shape[2]
    flat = piece.reshape(rows, count)
    gate = jnp.dot(flat, gate_weight, preferred_element_type=jnp.float32)
    up = jnp.dot(flat, up_weight, preferred_element_type=jnp.float32)
    gate_rows, up_rows = (
        lax.psum_scatter(gate, "gy", scatter_dimension=0, tiled=True),
        lax.psum_scatter(up, "gy", scatter_dimension=0, tiled=True),
    )
    return gated(gate_rows, up_rows)


def kernel(act, wg, wu, out, x, bg, bu, acc, got, res,
           act_sem, w_sem, send_sem, recv_sem, ex_send, ex_recv, out_sem):
    rows, width = act.shape
    depth = 2 * width
    half = rows // 2
    size = rows // CHUNKS
    part = size // 2
    tiles = acc.shape[0]
    gx = lax.axis_index("gx")
    c = lax.axis_index("gy")
    z = gx // 2
    col = gx % 2
    near = (PLANES - 1 - z) // 2
    p1 = z - 1 + 2 * near
    p3 = (PLANES - 1) * near
    p2 = 6 - z - p1 - p3
    order = [z, p1, p2, p3]

    def own(r, h):
        return pltpu.make_async_copy(
            act.at[pl.ds(h * half + r * part, part), :],
            x.at[z, pl.ds(r * size + h * part, part), pl.ds(col * width, width)],
            act_sem.at[r, h],
        )

    for r in range(CHUNKS):
        for h in range(2):
            own(r, h).start()

    def weights(s):
        span = pl.ds(order[s] * depth, depth)
        return [
            pltpu.make_async_copy(wg.at[span, :], bg.at[s % 2], w_sem.at[0, s]),
            pltpu.make_async_copy(wu.at[span, :], bu.at[s % 2], w_sem.at[1, s]),
        ]

    for s in range(2):
        for copy in weights(s):
            copy.start()

    targets = [z * 2 + (1 - col), gx + 2, gx - 2]
    barrier = pltpu.get_barrier_semaphore()
    pl.semaphore_signal(barrier, inc=1, device_id={"gx": targets[0]}, device_id_type=MESH)
    pl.semaphore_signal(barrier, inc=1, device_id={"gy": 1 - c}, device_id_type=MESH)

    @pl.when(z < PLANES - 1)
    def _():
        pl.semaphore_signal(barrier, inc=1, device_id={"gx": targets[1]}, device_id_type=MESH)

    @pl.when(z > 0)
    def _():
        pl.semaphore_signal(barrier, inc=1, device_id={"gx": targets[2]}, device_id_type=MESH)

    pl.semaphore_wait(barrier, 2 + (z + 2) // 3 + (5 - z) // 3)

    def link(d, p, side, r):
        block = x.at[p, pl.ds(r * size, size), pl.ds(side * width, width)]
        b = p * 2 + side
        return pltpu.make_async_remote_copy(
            src_ref=block, dst_ref=block,
            send_sem=send_sem.at[d, b, r], recv_sem=recv_sem.at[b, r],
            device_id={"gx": targets[d]}, device_id_type=MESH,
        )

    def along(at, p, r):
        inner = ((at == 1) & (p == 0)) | ((at == 2) & (p == 3))
        outer = ((at == 0) & (p == 1)) | ((at == 3) & (p == 2))
        return inner | (outer & (r % 2 == 1))

    def routes(p, side_own, r):
        rise = (p <= z) & (z < PLANES - 1)
        fall = (p >= z) & (z > 0)
        if side_own:
            return [(1, rise), (2, fall), (0, jnp.logical_not(along(z, p, r)))]
        return [(1, rise & along(z + 1, p, r)), (2, fall & along(z - 1, p, r))]

    def forward(p, side_own, r, wait=False):
        side = col if side_own else 1 - col
        for d, cond in routes(p, side_own, r):
            @pl.when(cond)
            def _(d=d):
                if wait:
                    link(d, p, side, r).wait_send()
                else:
                    link(d, p, side, r).start()

    def arrive(p, side_own, r):
        link(0, p, col if side_own else 1 - col, r).wait_recv()

    for r in range(CHUNKS):
        for h in range(2):
            own(r, h).wait()
        forward(z, True, r)

    def accumulate(s, first, count, span):
        here = pl.ds(first, count)
        for j in span:
            lhs = x[order[s], here, :]
            cut = pl.ds(j * TILE, TILE)
            gate = jnp.dot(lhs, bg[s % 2, :, cut], preferred_element_type=jnp.float32)
            up = jnp.dot(lhs, bu[s % 2, :, cut], preferred_element_type=jnp.float32)
            if s:
                acc[j, here, :TILE] += gate
                acc[j, here, TILE:] += up
            else:
                acc[j, here, :TILE] = gate
                acc[j, here, TILE:] = up

    def exchange(r, j):
        return pltpu.make_async_remote_copy(
            src_ref=acc.at[j, pl.ds(r * size + (1 - c) * part, part), :],
            dst_ref=got.at[j, pl.ds(r * part, part), :],
            send_sem=ex_send.at[j, r], recv_sem=ex_recv.at[j, r],
            device_id={"gy": 1 - c}, device_id_type=MESH,
        )

    def write(r):
        span = pl.ds(r * part, part)
        return pltpu.make_async_copy(res.at[span, :], out.at[span, :], out_sem.at[r])

    def finish(r):
        def body(j, carry):
            exchange(r, j).wait_recv()
            both = acc[j, pl.ds(r * size + c * part, part), :] + got[j, pl.ds(r * part, part), :]
            cut = pl.ds(pl.multiple_of(j * TILE, TILE), TILE)
            res[pl.ds(r * part, part), cut] = gated(both[:, :TILE], both[:, TILE:])
            return carry

        lax.fori_loop(0, tiles, body, 0)
        write(r).start()

    group = 1
    for s in range(PLANES):
        for copy in weights(s):
            copy.wait()

        def chunk(r, carry, s=s):
            if s < PLANES - 1:
                arrive(order[s + 1], True, r)
                forward(order[s + 1], True, r)
            arrive(order[s], False, r)
            forward(order[s], False, r)
            return carry

        if s < PLANES - 1:
            def block(k, carry, s=s):
                for i in range(group):
                    chunk(k * group + i, 0, s)
                accumulate(s, pl.multiple_of(k * group * size, size), group * size, range(tiles))
                return carry

            lax.fori_loop(0, CHUNKS // group, block, 0)
            if s + 2 < PLANES:
                for copy in weights(s + 2):
                    copy.start()
        else:
            def last(r, carry, s=s):
                chunk(r, 0, s)
                def push(j, carry):
                    exchange(r, j).start()
                    return carry

                for lo in range(0, tiles, SPAN):
                    hi = min(lo + SPAN, tiles)
                    accumulate(s, pl.multiple_of(r * size, size), size, range(lo, hi))
                    lax.fori_loop(lo, hi, push, 0)

                @pl.when(r > 0)
                def _():
                    finish(r - 1)
                return carry

            lax.fori_loop(0, CHUNKS, last, 0)
            finish(CHUNKS - 1)

    def drain(r, carry):
        for s in range(PLANES):
            forward(order[s], True, r, wait=True)
            forward(order[s], False, r, wait=True)

        def body(j, carry):
            exchange(r, j).wait_send()
            return carry

        lax.fori_loop(0, tiles, body, 0)
        write(r).wait()
        return carry

    lax.fori_loop(0, CHUNKS, drain, 0)


def fused(activations, gate_weight, up_weight):
    rows, _, width = activations.shape
    hidden = gate_weight.shape[1]
    tiles = hidden // TILE
    depth = 2 * width
    return pl.pallas_call(
        kernel,
        out_shape=jax.ShapeDtypeStruct((rows // 2, hidden), jnp.bfloat16),
        in_specs=[pl.BlockSpec(memory_space=pl.ANY)] * 3,
        out_specs=pl.BlockSpec(memory_space=pl.ANY),
        scratch_shapes=[
            pltpu.VMEM((PLANES, rows, depth), jnp.bfloat16),
            pltpu.VMEM((2, depth, hidden), jnp.bfloat16),
            pltpu.VMEM((2, depth, hidden), jnp.bfloat16),
            pltpu.VMEM((tiles, rows, 2 * TILE), jnp.float32),
            pltpu.VMEM((tiles, rows // 2, 2 * TILE), jnp.float32),
            pltpu.VMEM((rows // 2, hidden), jnp.bfloat16),
            pltpu.SemaphoreType.DMA((CHUNKS, 2)),
            pltpu.SemaphoreType.DMA((2, PLANES)),
            pltpu.SemaphoreType.DMA((3, 2 * PLANES, CHUNKS)),
            pltpu.SemaphoreType.DMA((2 * PLANES, CHUNKS)),
            pltpu.SemaphoreType.DMA((tiles, CHUNKS)),
            pltpu.SemaphoreType.DMA((tiles, CHUNKS)),
            pltpu.SemaphoreType.DMA((CHUNKS,)),
        ],
        compiler_params=pltpu.CompilerParams(
            collective_id=0, has_side_effects=True, vmem_limit_bytes=62 * 1024 * 1024
        ),
        cost_estimate=pl.CostEstimate(
            flops=4 * rows * PLANES * depth * hidden,
            bytes_accessed=4 * PLANES * depth * hidden,
            transcendentals=rows // 2 * hidden,
        ),
    )(activations.reshape(rows, width), gate_weight, up_weight)


def solution(mesh):
    def local(activations, gate_weight, up_weight):
        rows, _, width = activations.shape
        hidden = gate_weight.shape[1]
        fits = (
            mesh.shape["gx"] == 2 * PLANES and mesh.shape["gy"] == 2
            and width % 128 == 0 and hidden % TILE == 0 and rows % (32 * CHUNKS) == 0
        )
        return (fused if fits else shards)(activations, gate_weight, up_weight)

    placed = (P("groups", "gy", "gx"), P("gy", "gx"), P("gy", "gx"))
    return jax.shard_map(
        local, mesh=mesh, in_specs=placed, out_specs=P(("groups", "gy"), "gx"), check_vma=False
    )
```
